32 devices in a mesh: tile: 4 (over z), train: 8 (over y, x, core).
Axes of the slice: x: 2, y: 2, z: 4, core: 2. Of those that a mesh axis runs over, the one named last changes fastest.
Arguments:
- columns: bfloat16 [32768, 512], P(('tile', 'train')), may hold values from -6 to 6
- truth: bfloat16 [32768, 128], P(('tile', 'train')), may hold values from -6 to 6
- weight_in: bfloat16 [512, 1024], replicated, may hold values from -0.25 to 0.25
- weight_out: bfloat16 [1024, 128], replicated, may hold values from -0.1875 to 0.1875
- master_in: float32 [512, 1024], P(None, 'tile'), may hold values from -0.25 to 0.25
- master_out: float32 [1024, 128], P('tile'), may hold values from -0.1875 to 0.1875
- moment_in: float32 [512, 1024], P(None, 'tile'), may hold values from -6 to 6
- moment_out: float32 [1024, 128], P('tile'), may hold values from -6 to 6
- second_in: float32 [512, 1024], P(None, 'tile'), may hold values from 1 to 30
- second_out: float32 [1024, 128], P('tile'), may hold values from 1 to 30
- counts: int32 [32], P(('tile', 'train')), may hold values from 1 to 16, as said below
- sampled: int32 [512, 128], P(('tile', 'train')), may hold values from 0 to 1023
- routes: int32 [512, 1], P(('tile', 'train')), may hold values from 0 to 7; in each aligned block of 16 rows (0 to 15, 16 to 31, ...) at most 2 rows name the same one
Outputs:
- predicted: bfloat16 [32768, 128], P(('tile', 'train'))
- trainer_loss: float32 [32], P(('tile', 'train'))
- fresh_in: bfloat16 [512, 1024], replicated
- fresh_out: bfloat16 [1024, 128], replicated
- new_master_in: float32 [512, 1024], P(None, 'tile')
- new_master_out: float32 [1024, 128], P('tile')
- new_moment_in: float32 [512, 1024], P(None, 'tile')
- new_moment_out: float32 [1024, 128], P('tile')
- new_second_in: float32 [512, 1024], P(None, 'tile')
- new_second_out: float32 [1024, 128], P('tile')
The draws below stay inside these ranges and needn't reach their ends.
Inputs may be any that keep to these rules, and one draw needn't show every extreme that they name: `counts`: one device's count reaches 16; the others are at most 10. `routes`: among the 16 slots of one device every trainer is named by exactly 2 slots.
All inputs are finite; a program needn't handle non-finite values.
Results may differ from the reference program's by a relative error of at most 0.0049.
Values may be sent and summed in bfloat16 or wider, within the bound.
A program may use at most 64 MiB of HBM per device.

```python
import math
import jax
import jax.numpy as jnp
import numpy as np
from jax import lax

IN_FEAT = 512
HIDDEN_SIZE = 1024
OUT_FEAT = 128
COLS_DEV = 1024
BLK = 128
CAP = 2
SLOTS = 16
COLUMNS = 32768
BLOCKS = 512
N_TILE = 4
N_TRAIN = 8


def draw_counts(key, part):
    key = jax.random.fold_in(key, 11)
    first, second = jax.random.split(key)
    nodes = N_TILE * N_TRAIN
    slots = N_TRAIN * CAP
    values = jax.random.randint(first, (nodes,), 1, 2 * slots // 3 + 1)
    heavy = jax.random.randint(second, (), 0, nodes)
    return jnp.where(jnp.arange(nodes) == heavy, slots, values).astype(jnp.int32)


def plant(drawn, key, smallest, largest):
    place = [jax.random.randint(jax.random.fold_in(key, axis), (), 0, length) for axis, length in enumerate(drawn.shape)]
    main_axis = drawn.shape.index(max(drawn.shape))
    beside = place[:main_axis] + [(place[main_axis] + 1) % drawn.shape[main_axis]] + place[main_axis + 1:]
    return drawn.at[tuple(place)].set(smallest).at[tuple(beside)].set(largest)


def steps_of(own_key, extent, cuts, smallest, high):
    factor_of, own = 1.0, jax.random.fold_in(own_key, 6)
    for dim, blocks in cuts:
        draws = jnp.exp(jax.random.uniform(jax.random.fold_in(own, dim), (blocks,), jnp.float32, smallest / len(cuts), high / len(cuts)))
        factor_of = factor_of * jnp.repeat(draws, extent[dim] // blocks).reshape([-1 if axis == dim else 1 for axis in range(len(extent))])
    return factor_of


def routed_block(rng, own, number, rows, amount, top, most, skew):
    order = jax.random.permutation(rng, amount)
    packed, common = shares(amount, rows * top, most, skew, True), shares(amount, rows * top, most, skew, False)
    places = jnp.arange(amount)

    def named(lengths, offset_by):
        used = int((lengths > 0).sum())
        fixed = max(1, used // 4)
        passed = fixed + (places - fixed + offset_by * (used - fixed)) % max(1, amount - fixed)
        return jnp.zeros((amount,), jnp.int32).at[order[jnp.where(places < fixed, places, passed)]].set(jnp.asarray(lengths, jnp.int32))

    lengths = jnp.where(number % 4 == 0, named(packed, number // 4), named(common, number - number // 4 - 1))
    mixed = jax.random.permutation(jax.random.fold_in(own, 3), amount)
    giver, sink = mixed[0:amount // 2 * 2:2], mixed[1:amount // 2 * 2:2]
    room = jnp.minimum(lengths[giver] - 1, most - lengths[sink]) // 2
    room = jnp.where((giver == order[0]) | (sink == order[0]) | (lengths[sink] == 0), 0, jnp.maximum(room, 0))
    passed = jax.random.randint(jax.random.fold_in(own, 4), (amount // 2,), 0, 1 << 20) % (room + 1)
    lengths = lengths.at[giver].add(-passed).at[sink].add(passed)
    items = jnp.searchsorted(jnp.cumsum(lengths), jnp.arange(rows * top), side="right").astype(jnp.int32)
    table = items.reshape(top, rows).T
    table = table[jax.random.permutation(jax.random.fold_in(own, 1), rows)]
    offset_by = jax.random.randint(jax.random.fold_in(own, 2), (rows, 1), 0, top)
    return jnp.take_along_axis(table, (jnp.arange(top)[None, :] + offset_by) % top, axis=1)


def shares(count, total, limit, skew, full):
    loads = [(1 << 20) // math.isqrt(rank ** skew) + 1 for rank in range(1, count + 1)]
    largest = limit if full else min(limit, max(-(-total // count), total * loads[0] // sum(loads)))
    least = 1 if total - largest >= count - 1 else 0
    holding, rest = [largest] + [least] * (count - 1), total - largest - least * (count - 1)
    while rest > 0:
        movable = [i for i in range(1, count) if holding[i] < largest] or [i for i in range(1, count) if holding[i] < limit]
        mass, left = sum([loads[i] for i in movable]), rest
        for i in movable:
            addition = min(limit - holding[i], max(1, left * loads[i] // mass), rest)
            holding[i] = holding[i] + addition
            rest = rest - addition
    return np.array(holding)


def normal_values(key, shape, spread, most, shards=(), kind=jnp.bfloat16):
    array = spread * jax.random.normal(key, shape, jnp.float32)
    if shards:
        array = array * steps_of(key, shape, shards, -0.22, 0.18)
    return jnp.clip(array, -most, most).astype(kind)


def setup_inputs(seed: int = 0) -> dict:
    seeds = jax.random.split(jax.random.key(seed), 14)
    columns = normal_values(seeds[0], (COLUMNS, IN_FEAT), 1.0, 6.0, ((0, 32),))
    truth = normal_values(seeds[1], (COLUMNS, OUT_FEAT), 1.0, 6.0, ((0, 32),))
    weight_in = normal_values(seeds[2], (IN_FEAT, HIDDEN_SIZE), IN_FEAT ** -0.5, 0.25)
    weight_out = normal_values(seeds[3], (HIDDEN_SIZE, OUT_FEAT), HIDDEN_SIZE ** -0.5, 0.1875)
    master_in = normal_values(seeds[4], (IN_FEAT, HIDDEN_SIZE), IN_FEAT ** -0.5, 0.25, ((1, 4),), jnp.float32)
    master_out = normal_values(seeds[5], (HIDDEN_SIZE, OUT_FEAT), HIDDEN_SIZE ** -0.5, 0.1875, ((0, 4),), jnp.float32)
    moment_in = normal_values(seeds[6], (IN_FEAT, HIDDEN_SIZE), 1.0, 6.0, ((1, 4),), jnp.float32)
    moment_out = normal_values(seeds[7], (HIDDEN_SIZE, OUT_FEAT), 1.0, 6.0, ((0, 4),), jnp.float32)
    second_in = jnp.clip(jnp.exp(math.log(30.0) - 3.4011974 * jax.random.uniform(seeds[8], (IN_FEAT, HIDDEN_SIZE), jnp.float32) ** steps_of(seeds[8], (IN_FEAT, HIDDEN_SIZE), ((1, 4),), -0.2, 0.2)), 1.0, 30.0)
    second_out = jnp.clip(jnp.exp(math.log(30.0) - 3.4011974 * jax.random.uniform(seeds[9], (HIDDEN_SIZE, OUT_FEAT), jnp.float32) ** steps_of(seeds[9], (HIDDEN_SIZE, OUT_FEAT), ((0, 4),), -0.2, 0.2)), 1.0, 30.0)
    counts = draw_counts(jax.random.fold_in(seeds[13], 71), 0)
    sampled = plant(jax.random.randint(seeds[11], (BLOCKS, BLK), 0, COLS_DEV), jax.random.fold_in(seeds[11], 1), 0, COLS_DEV - 1).astype(jnp.int32)
    routes_keys = jax.random.split(jax.random.fold_in(seeds[12], 1), BLOCKS // SLOTS)
    routes_turns = jax.random.permutation(jax.random.fold_in(seeds[12], 3), BLOCKS // SLOTS)
    routes = jax.vmap(lambda own, number: routed_block(jax.random.fold_in(seeds[12], 2), own, number, SLOTS, N_TRAIN, 1, CAP, 0))(routes_keys, routes_turns).reshape((BLOCKS, 1))
    return dict(columns=columns, truth=truth, weight_in=weight_in, weight_out=weight_out, master_in=master_in, master_out=master_out, moment_in=moment_in, moment_out=moment_out, second_in=second_in, second_out=second_out, counts=counts, sampled=sampled, routes=routes)


rate = 0.001
first_fix = 1.0 - 0.9 ** 8
second_fix = 1.0 - 0.999 ** 8

def silu_slope(pre):
    sig = jax.nn.sigmoid(pre)
    return sig * (1.0 + pre * (1.0 - sig))

def block_pass(rows_in, rows_want, weight_in, weight_out):
    pre = jnp.dot(rows_in, weight_in, preferred_element_type=jnp.float32)
    hidden = jax.nn.silu(pre).astype(jnp.bfloat16)
    output = jnp.dot(hidden, weight_out, preferred_element_type=jnp.float32)
    error = output - rows_want.astype(jnp.float32)
    back = error.astype(jnp.bfloat16)
    grad_out = jnp.dot(hidden.T, back, preferred_element_type=jnp.float32)
    hidden_grad = jnp.dot(back, weight_out.T, preferred_element_type=jnp.float32)
    pre_grad = (hidden_grad * silu_slope(pre)).astype(jnp.bfloat16)
    grad_in = jnp.dot(rows_in.T, pre_grad, preferred_element_type=jnp.float32)
    return (grad_in, grad_out, jnp.sum(error * error))

def adam_update(master, moment, second, grad):
    moment = 0.9 * moment + 0.1 * grad
    second = 0.999 * second + 0.001 * grad * grad
    master = master - rate * (moment / first_fix) / (jnp.sqrt(second / second_fix) + 1e-08)
    return (master, moment, second)

def reference(columns, truth, weight_in, weight_out, master_in, master_out, moment_in, moment_out, second_in, second_out, counts, sampled, routes):
    nodes = N_TILE * N_TRAIN
    slots = N_TRAIN * CAP
    inference_hidden = jax.nn.silu(jnp.dot(columns, weight_in, preferred_element_type=jnp.float32)).astype(jnp.bfloat16)
    predicted = jnp.dot(inference_hidden, weight_out, preferred_element_type=jnp.float32).astype(jnp.bfloat16)

    def per_device(carry, rank):
        local_in = lax.dynamic_slice_in_dim(columns, rank * COLS_DEV, COLS_DEV, 0)
        local_want = lax.dynamic_slice_in_dim(truth, rank * COLS_DEV, COLS_DEV, 0)
        picks = lax.dynamic_slice_in_dim(sampled, rank * slots, slots, 0)
        owners = lax.dynamic_slice_in_dim(routes, rank * slots, slots, 0)[:, 0]
        base = rank // N_TRAIN * N_TRAIN

        def per_block(block, inner):
            grad_in, grad_out, losses = inner
            rows = picks[block]
            part_in, part_out, loss = block_pass(local_in[rows], local_want[rows], weight_in, weight_out)
            losses = losses.at[base + owners[block]].add(loss)
            return (grad_in + part_in, grad_out + part_out, losses)
        return (lax.fori_loop(jnp.int32(0), counts[rank], per_block, carry), None)
    start = (jnp.zeros((IN_FEAT, HIDDEN_SIZE), jnp.float32), jnp.zeros((HIDDEN_SIZE, OUT_FEAT), jnp.float32), jnp.zeros((nodes,), jnp.float32))
    (grad_in, grad_out, losses), _ = lax.scan(per_device, start, jnp.arange(nodes, dtype=jnp.int32))
    trainer_loss = losses / (BLK * OUT_FEAT)
    scale = 2.0 / BLK
    new_master_in, new_moment_in, new_second_in = adam_update(master_in, moment_in, second_in, scale * grad_in)
    new_master_out, new_moment_out, new_second_out = adam_update(master_out, moment_out, second_out, scale * grad_out)
    return (predicted, trainer_loss, new_master_in.astype(jnp.bfloat16), new_master_out.astype(jnp.bfloat16), new_master_in, new_master_out, new_moment_in, new_moment_out, new_second_in, new_second_out)
```

```python
import jax
import jax.numpy as jnp
from jax import lax
from jax.sharding import PartitionSpec as P

BLK = 128


rate = 0.001
first_fix = 1.0 - 0.9**8
second_fix = 1.0 - 0.999**8


def silu_slope(pre):
    sig = jax.nn.sigmoid(pre)
    return sig * (1.0 + pre * (1.0 - sig))


def adam_update(master, moment, second, grad):
    moment = 0.9 * moment + 0.1 * grad
    second = 0.999 * second + 0.001 * grad * grad
    master = master - rate * (moment / first_fix) / (jnp.sqrt(second / second_fix) + 1e-08)
    return (master, moment, second)


def local(
    columns,
    truth,
    weight_in,
    weight_out,
    master_in,
    master_out,
    moment_in,
    moment_out,
    second_in,
    second_out,
    counts,
    sampled,
    routes,
):
    f32 = jnp.float32
    trainers = lax.axis_size("train")
    live = jnp.arange(sampled.shape[0], dtype=jnp.int32) < counts[0]
    named = routes == jnp.arange(trainers, dtype=jnp.int32)[None, :]
    kinds = jnp.concatenate([named & live[:, None], live[:, None]], axis=1)
    hit = sampled.reshape(1, -1) == jnp.arange(columns.shape[0], dtype=jnp.int32)[:, None]
    times = jnp.dot(
        hit.astype(jnp.bfloat16),
        jnp.repeat(kinds, BLK, axis=0).astype(jnp.bfloat16),
        preferred_element_type=f32,
    )
    pre = jnp.dot(columns, weight_in, preferred_element_type=f32)
    hidden = jax.nn.silu(pre).astype(jnp.bfloat16)
    output = jnp.dot(hidden, weight_out, preferred_element_type=f32)
    predicted = output.astype(jnp.bfloat16)
    error = output - truth.astype(f32)
    squares = jnp.sum(error * error, axis=1, keepdims=True)
    losses = lax.psum(jnp.sum(squares * times[:, :trainers], axis=0), "train")
    me = lax.axis_index("train")
    trainer_loss = lax.dynamic_slice_in_dim(losses, me, 1) / (BLK * weight_out.shape[1])
    often = times[:, trainers:]
    hidden_grad = jnp.dot(error.astype(jnp.bfloat16), weight_out.T, preferred_element_type=f32)
    pre_grad = (often * hidden_grad * silu_slope(pre)).astype(jnp.bfloat16)
    grad_in = jnp.dot(columns.T, pre_grad, preferred_element_type=f32)
    grad_out = jnp.dot(hidden.T, (often * error).astype(jnp.bfloat16), preferred_element_type=f32)
    scale = 2.0 / BLK
    share_in = lax.psum_scatter(grad_in, "tile", scatter_dimension=1, tiled=True)
    share_out = lax.psum_scatter(grad_out, "tile", scatter_dimension=0, tiled=True)
    share_in, share_out = lax.psum((share_in, share_out), "train")
    new_master_in, new_moment_in, new_second_in = adam_update(
        master_in, moment_in, second_in, scale * share_in
    )
    new_master_out, new_moment_out, new_second_out = adam_update(
        master_out, moment_out, second_out, scale * share_out
    )
    rounded_in = new_master_in.astype(jnp.bfloat16)
    rounded_out = new_master_out.astype(jnp.bfloat16)
    fresh_in, fresh_out = (
        lax.all_gather(rounded_in, "tile", axis=1, tiled=True),
        lax.all_gather(rounded_out, "tile", axis=0, tiled=True),
    )
    return (
        predicted,
        trainer_loss,
        fresh_in,
        fresh_out,
        new_master_in,
        new_master_out,
        new_moment_in,
        new_moment_out,
        new_second_in,
        new_second_out,
    )


def solution(mesh):
    return jax.shard_map(
        local,
        mesh=mesh,
        in_specs=(
            P(("tile", "train"), None),
            P(("tile", "train"), None),
            P(),
            P(),
            P(None, "tile"),
            P("tile", None),
            P(None, "tile"),
            P("tile", None),
            P(None, "tile"),
            P("tile", None),
            P(("tile", "train")),
            P(("tile", "train"), None),
            P(("tile", "train"), None),
        ),
        out_specs=(
            P(("tile", "train"), None),
            P(("tile", "train")),
            P(),
            P(),
            P(None, "tile"),
            P("tile", None),
            P(None, "tile"),
            P("tile", None),
            P(None, "tile"),
            P("tile", None),
        ),
        check_vma=False,
    )
```

```python
import functools
import jax
import jax.numpy as jnp
from jax import lax
from jax.experimental import pallas as pl
from jax.experimental.pallas import tpu as pltpu
from jax.sharding import PartitionSpec as P

BLK = 128
LANES = 128
STREAMS = 2
CHUNK = 256

rate = 0.001
first_fix = 1.0 - 0.9**8
second_fix = 1.0 - 0.999**8
f32, bf16 = jnp.float32, jnp.bfloat16


def adam_update(master, moment, second, grad):
    moment = 0.9 * moment + 0.1 * grad
    second = 0.999 * second + 0.001 * grad * grad
    master = master - rate * (moment / first_fix) / (jnp.sqrt(second / second_fix) + 1e-08)
    return (master, moment, second)


def bits_of(size):
    return size.bit_length() - 1


def stream_orders(trainers):
    ascending = list(range(bits_of(trainers)))
    return [ascending, ascending[:1] + ascending[:0:-1]]


def place_of(index, order):
    place = 0
    for bit in order:
        place = place * 2 + (index // 2**bit) % 2
    return place


def kernel(
    tiles, trainers,
    columns, truth, weight_in, weight_out,
    master_in, master_out, moment_in, moment_out, second_in, second_out,
    counts, sampled, routes,
    predicted, trainer_loss, fresh_in, fresh_out,
    new_master_in, new_master_out, new_moment_in, new_moment_out, new_second_in, new_second_out,
    marks, pre_grads, hiddens, backs, loss_rows,
    total, outgoing, arrived_train, arrived_tile, gathered, fresh, loss_out, loss_in,
    send_sem, recv_sem,
):
    t, u = lax.axis_index("tile"), lax.axis_index("train")
    train_bits, tile_bits = bits_of(trainers), bits_of(tiles)
    orders = stream_orders(trainers)
    tile_order = list(range(tile_bits))
    piece = total.shape[3]
    share_rows = STREAMS * trainers * piece
    feat, width = master_in.shape
    height = master_out.shape[0]
    blocks_in = width // LANES

    def bit_of(axis, bit):
        return ((u if axis == "train" else t) // 2**bit) % 2

    def partner(axis, bit):
        index = u if axis == "train" else t
        return {axis: index + 2**bit * (1 - 2 * bit_of(axis, bit))}

    barrier = pltpu.get_barrier_semaphore()
    for axis, number in (("train", train_bits), ("tile", tile_bits)):
        for bit in range(number):
            pl.semaphore_signal(
                barrier, inc=1, device_id=partner(axis, bit), device_id_type=pl.DeviceIdType.MESH
            )

    slots = sampled.shape[0]
    lane = lax.broadcasted_iota(jnp.int32, (slots, LANES), 1)
    slot = lax.broadcasted_iota(jnp.int32, (slots, LANES), 0)
    named = (lane >= trainers) | (routes[...] == lane)
    kinds = jnp.where(named & (slot < counts[...]), 1.0, 0.0).astype(f32)
    for b in range(slots):
        marks[b * BLK : (b + 1) * BLK, :] = jnp.broadcast_to(
            kinds[b : b + 1, :], (BLK, LANES)
        ).astype(bf16)
    loss_rows[...] = jnp.zeros_like(loss_rows)

    def chunk(step, carry):
        start = pl.multiple_of(step * CHUNK, CHUNK)
        rows = pl.ds(start, CHUNK)
        own = lax.broadcasted_iota(jnp.int32, (CHUNK, LANES), 0) + start
        hits = jnp.concatenate(
            [jnp.where(own == sampled[b : b + 1, :], 1.0, 0.0).astype(bf16) for b in range(slots)],
            axis=1,
        )
        times = jnp.dot(hits, marks[...], preferred_element_type=f32)
        pre = jnp.dot(columns[rows, :], weight_in[...], preferred_element_type=f32)
        sig = 0.5 + 0.5 * jnp.tanh(0.5 * pre)
        value = pre * sig
        hidden = value.astype(bf16)
        hiddens[rows, :] = hidden
        output = jnp.dot(hidden, weight_out[...], preferred_element_type=f32)
        predicted[rows, :] = output.astype(bf16)
        error = output - truth[rows, :].astype(f32)
        squares = jnp.sum(error * error, axis=1, keepdims=True)
        loss_rows[...] += jnp.sum((squares * times).reshape(CHUNK // 8, 8, LANES), axis=0)
        often = times[:, LANES - 1 :]
        backs[rows, :] = (often * error).astype(bf16)
        hidden_grad = lax.dot_general(
            error.astype(bf16), weight_out[...], (((1,), (1,)), ((), ())),
            preferred_element_type=f32,
        )
        pre_grads[rows, :] = (often * hidden_grad * (sig + value * (1.0 - sig))).astype(bf16)
        return carry

    lax.fori_loop(0, columns.shape[0] // CHUNK, chunk, 0)

    for tile in range(tiles):
        place = place_of(tile, tile_order)
        across = slice(tile * width, (tile + 1) * width)
        part_in = lax.dot_general(
            columns[...], pre_grads[:, across], (((0,), (0,)), ((), ())),
            preferred_element_type=f32,
        )
        part_out = lax.dot_general(
            hiddens[:, tile * height : (tile + 1) * height], backs[...], (((0,), (0,)), ((), ())),
            preferred_element_type=f32,
        )
        parts = [part_in[:, c * LANES : (c + 1) * LANES] for c in range(blocks_in)] + [part_out]
        missing = share_rows - blocks_in * feat - height
        if missing:
            parts.append(jnp.zeros((missing, LANES), f32))
        total[:, :, place] = jnp.concatenate(parts, axis=0).reshape(
            STREAMS, trainers, piece, LANES
        )

    pl.semaphore_wait(barrier, train_bits + tile_bits)

    used = [0]
    pending = []

    def send(source, target, axis, bit):
        number = used[0]
        used[0] += 1
        copy = pltpu.make_async_remote_copy(
            src_ref=source,
            dst_ref=target,
            send_sem=send_sem.at[number],
            recv_sem=recv_sem.at[number],
            device_id=partner(axis, bit),
            device_id_type=pl.DeviceIdType.MESH,
        )
        copy.start()
        pending.append(copy)
        return copy

    starts = [0] * STREAMS
    flying = [None] * STREAMS
    losses = loss_rows[...]
    loss_copy = None
    for step in range(train_bits):
        half = 2 ** (train_bits - 1 - step)
        if loss_copy is not None:
            loss_copy.wait_recv()
            losses = losses + loss_in[step - 1]
        loss_out[step] = losses
        loss_copy = send(loss_out.at[step], loss_in.at[step], "train", step)
        for s in range(STREAMS):
            if step:
                flying[s].wait_recv()
                total[s, pl.ds(starts[s], 2 * half)] += arrived_train[s, 2 * half : 4 * half].astype(f32)
            bit = orders[s][step]
            mine = bit_of("train", bit)
            away = pl.ds(starts[s] + (1 - mine) * half, half)
            outgoing[s, away] = total[s, away].astype(bf16)
            flying[s] = send(
                outgoing.at[s, away], arrived_train.at[s, pl.ds(half, half)], "train", bit
            )
            starts[s] = starts[s] + mine * half
    loss_copy.wait_recv()
    losses = losses + loss_in[train_bits - 1]
    mine_only = lax.broadcasted_iota(jnp.int32, losses.shape, 1) == u
    trainer_loss[...] = jnp.sum(
        jnp.where(mine_only, losses, 0.0), axis=(0, 1), keepdims=True
    ) / (BLK * weight_out.shape[1])

    spots = [0] * STREAMS
    for step in range(tile_bits):
        half = 2 ** (tile_bits - 1 - step)
        for s in range(STREAMS):
            flying[s].wait_recv()
            if step == 0:
                total[s, starts[s]] += arrived_train[s, 1].astype(f32)
            else:
                total[s, starts[s], pl.ds(spots[s], 2 * half)] += arrived_tile[
                    s, 2 * half : 4 * half
                ].astype(f32)
            bit = tile_order[step]
            mine = bit_of("tile", bit)
            away = pl.ds(spots[s] + (1 - mine) * half, half)
            outgoing[s, starts[s], away] = total[s, starts[s], away].astype(bf16)
            flying[s] = send(
                outgoing.at[s, starts[s], away], arrived_tile.at[s, pl.ds(half, half)], "tile", bit
            )
            spots[s] = spots[s] + mine * half

    begin = [None] * STREAMS
    for s in range(STREAMS):
        flying[s].wait_recv()
        done = total[s, starts[s], spots[s]] + arrived_tile[s, 1].astype(f32)
        gathered[s, starts[s]] = done.astype(bf16)
        begin[s] = starts[s]
    for step in reversed(range(train_bits)):
        size = 2 ** (train_bits - 1 - step)
        for s in range(STREAMS):
            if step < train_bits - 1:
                flying[s].wait_recv()
                begin[s] = begin[s] - bit_of("train", orders[s][step + 1]) * (size // 2)
            region = gathered.at[s, pl.ds(begin[s], size)]
            flying[s] = send(region, region, "train", orders[s][step])
    for s in range(STREAMS):
        flying[s].wait_recv()

    grads = gathered[...].reshape(share_rows, LANES)
    scale = 2.0 / BLK
    shares = []
    for c in range(blocks_in):
        across = slice(c * LANES, (c + 1) * LANES)
        grad = scale * grads[c * feat : (c + 1) * feat].astype(f32)
        master, moment, second = adam_update(
            master_in[:, across], moment_in[:, across], second_in[:, across], grad
        )
        new_master_in[:, across] = master
        new_moment_in[:, across] = moment
        new_second_in[:, across] = second
        shares.append(master.astype(bf16))
    grad = scale * grads[blocks_in * feat : blocks_in * feat + height].astype(f32)
    master, moment, second = adam_update(master_out[...], moment_out[...], second_out[...], grad)
    new_master_out[...] = master
    new_moment_out[...] = moment
    new_second_out[...] = second
    shares.append(master.astype(bf16))
    missing = share_rows - blocks_in * feat - height
    if missing:
        shares.append(jnp.zeros((missing, LANES), bf16))
    for copy in pending:
        copy.wait_send()
    pending.clear()
    gathered[...] = jnp.concatenate(shares, axis=0).reshape(gathered.shape)
    for s in range(STREAMS):
        fresh[s, starts[s], spots[s]] = gathered[s, starts[s]]
    begin = list(spots)
    for step in reversed(range(tile_bits)):
        size = 2 ** (tile_bits - 1 - step)
        for s in range(STREAMS):
            if step < tile_bits - 1:
                flying[s].wait_recv()
                begin[s] = begin[s] - bit_of("tile", tile_order[step + 1]) * (size // 2)
            region = fresh.at[s, starts[s], pl.ds(begin[s], size)]
            flying[s] = send(region, region, "tile", tile_order[step])
    begin = list(starts)
    for step in reversed(range(train_bits)):
        size = 2 ** (train_bits - 1 - step)
        for s in range(STREAMS):
            flying[s].wait_recv()
            if step < train_bits - 1:
                begin[s] = begin[s] - bit_of("train", orders[s][step + 1]) * (size // 2)
            region = fresh.at[s, pl.ds(begin[s], size)]
            flying[s] = send(region, region, "train", orders[s][step])
    for s in range(STREAMS):
        flying[s].wait_recv()
    for tile in range(tiles):
        flat = fresh[:, :, place_of(tile, tile_order)].reshape(share_rows, LANES)
        for c in range(blocks_in):
            left = tile * width + c * LANES
            fresh_in[:, left : left + LANES] = flat[c * feat : (c + 1) * feat]
        fresh_out[tile * height : (tile + 1) * height, :] = flat[
            blocks_in * feat : blocks_in * feat + height
        ]
    for copy in pending:
        copy.wait_send()


def local(
    columns, truth, weight_in, weight_out,
    master_in, master_out, moment_in, moment_out, second_in, second_out,
    counts, sampled, routes,
):
    tiles, trainers = lax.axis_size("tile"), lax.axis_size("train")
    train_bits, tile_bits = bits_of(trainers), bits_of(tiles)
    rows, feat = columns.shape
    hidden, outs = weight_out.shape
    slots = sampled.shape[0]
    needed = (feat * master_in.shape[1] + master_out.shape[0] * outs) // LANES
    piece = -(-needed // (STREAMS * trainers * 16)) * 16
    copies = (2 * STREAMS) * (train_bits + tile_bits) + STREAMS * train_bits + train_bits
    like = lambda a: jax.ShapeDtypeStruct(a.shape, a.dtype)
    results = pl.pallas_call(
        functools.partial(kernel, tiles, trainers),
        out_shape=(
            like(truth),
            jax.ShapeDtypeStruct((1, 1), f32),
            like(weight_in),
            like(weight_out),
            like(master_in), like(master_out),
            like(moment_in), like(moment_out),
            like(second_in), like(second_out),
        ),
        in_specs=[pl.BlockSpec(memory_space=pltpu.VMEM)] * 13,
        out_specs=(pl.BlockSpec(memory_space=pltpu.VMEM),) * 10,
        scratch_shapes=[
            pltpu.VMEM((slots * BLK, LANES), bf16),
            pltpu.VMEM((rows, hidden), bf16),
            pltpu.VMEM((rows, hidden), bf16),
            pltpu.VMEM((rows, outs), bf16),
            pltpu.VMEM((8, LANES), f32),
            pltpu.VMEM((STREAMS, trainers, tiles, piece, LANES), f32),
            pltpu.VMEM((STREAMS, trainers, tiles, piece, LANES), bf16),
            pltpu.VMEM((STREAMS, trainers, tiles, piece, LANES), bf16),
            pltpu.VMEM((STREAMS, tiles, piece, LANES), bf16),
            pltpu.VMEM((STREAMS, trainers, piece, LANES), bf16),
            pltpu.VMEM((STREAMS, trainers, tiles, piece, LANES), bf16),
            pltpu.VMEM((train_bits, 8, LANES), f32),
            pltpu.VMEM((train_bits, 8, LANES), f32),
            pltpu.SemaphoreType.DMA((copies,)),
            pltpu.SemaphoreType.DMA((copies,)),
        ],
        compiler_params=pltpu.CompilerParams(
            collective_id=0, has_side_effects=True, vmem_limit_bytes=48 * 2**20
        ),
    )(
        columns, truth, weight_in, weight_out,
        master_in, master_out, moment_in, moment_out, second_in, second_out,
        counts.reshape(1, 1), sampled, routes,
    )
    return (results[0], results[1].reshape(1)) + tuple(results[2:])


def solution(mesh):
    return jax.shard_map(
        local,
        mesh=mesh,
        in_specs=(
            P(("tile", "train"), None),
            P(("tile", "train"), None),
            P(),
            P(),
            P(None, "tile"),
            P("tile", None),
            P(None, "tile"),
            P("tile", None),
            P(None, "tile"),
            P("tile", None),
            P(("tile", "train")),
            P(("tile", "train"), None),
            P(("tile", "train"), None),
        ),
        out_specs=(
            P(("tile", "train"), None),
            P(("tile", "train")),
            P(),
            P(),
            P(None, "tile"),
            P("tile", None),
            P(None, "tile"),
            P("tile", None),
            P(None, "tile"),
            P("tile", None),
        ),
        check_vma=False,
    )
```

```python
import functools
import jax
import jax.numpy as jnp
from jax import lax
from jax.experimental import pallas as pl
from jax.experimental.pallas import tpu as pltpu
from jax.sharding import PartitionSpec as P

BLK = 128
LANES = 128
STREAMS = 2
CHUNK = 256

rate = 0.001
first_fix = 1.0 - 0.9**8
second_fix = 1.0 - 0.999**8
f32, bf16 = jnp.float32, jnp.bfloat16


def adam_update(master, moment, second, grad):
    moment = 0.9 * moment + 0.1 * grad
    second = 0.999 * second + 0.001 * grad * grad
    master = master - rate * (moment / first_fix) / (jnp.sqrt(second / second_fix) + 1e-08)
    return (master, moment, second)


def bits_of(size):
    return size.bit_length() - 1


def stream_orders(trainers):
    ascending = list(range(bits_of(trainers)))
    return [ascending, ascending[:1] + ascending[:0:-1]]


def kernel(
    tiles, trainers,
    columns_hbm, truth_hbm, weight_in_hbm, weight_out_hbm,
    master_in, master_out, moment_in, moment_out, second_in, second_out,
    sampled_hbm, counts, routes,
    predicted_hbm, trainer_loss, fresh_in_hbm, fresh_out_hbm,
    new_master_in, new_master_out, new_moment_in, new_moment_out, new_second_in, new_second_out,
    columns, truth, weight_in, weight_out, sampled, master, moment, second,
    predicted, fresh_in, fresh_out,
    marks, pre_grads, hiddens, backs, loss_rows,
    total, outgoing, arrived_train, arrived_tile, gathered, fresh, loss_out, loss_in,
    send_sem, recv_sem, load_sem, store_sem,
):
    t, u = lax.axis_index("tile"), lax.axis_index("train")
    train_bits = bits_of(trainers)
    orders = stream_orders(trainers)
    piece = total.shape[3]
    share_rows = STREAMS * trainers * piece
    feat, width = master_in.shape
    height = master_out.shape[0]
    blocks_in = width // LANES

    def load(source, target):
        copy = pltpu.make_async_copy(source, target, load_sem.at[len(loads)])
        copy.start()
        loads.append(copy)

    def store(source, target):
        copy = pltpu.make_async_copy(source, target, store_sem.at[len(stores)])
        copy.start()
        stores.append(copy)

    loads, stores = [], []
    load(sampled_hbm, sampled)
    load(columns_hbm, columns)
    load(weight_in_hbm, weight_in)
    load(weight_out_hbm, weight_out)
    load(truth_hbm, truth)
    first_loads = len(loads)
    end_in = blocks_in * feat
    for inner, outer, flat in (
        (master_in, master_out, master), (moment_in, moment_out, moment), (second_in, second_out, second)
    ):
        for c in range(blocks_in):
            load(inner.at[:, pl.ds(c * LANES, LANES)], flat.at[pl.ds(c * feat, feat)])
        load(outer, flat.at[pl.ds(end_in, height)])
        if end_in + height < share_rows:
            missing = share_rows - end_in - height
            flat[end_in + height :, :] = jnp.zeros((missing, LANES), f32)

    def bit_of(bit):
        return (u // 2**bit) % 2

    def partner(bit):
        return {"train": u + 2**bit * (1 - 2 * bit_of(bit))}

    def other_tile(distance):
        return {"tile": (t + distance) % tiles}

    friends = [partner(bit) for bit in range(train_bits)]
    friends += [other_tile(distance) for distance in range(1, tiles)]
    barrier = pltpu.get_barrier_semaphore()
    for friend in friends:
        pl.semaphore_signal(
            barrier, inc=1, device_id=friend, device_id_type=pl.DeviceIdType.MESH
        )

    slots = sampled.shape[0]
    lane = lax.broadcasted_iota(jnp.int32, (BLK, LANES), 1)
    for b in range(slots):
        named = (lane >= trainers) | (lane == routes[0, b])
        named = named & (counts[0] > b)
        marks[b * BLK : (b + 1) * BLK, :] = jnp.where(named, 1.0, 0.0).astype(bf16)
    for copy in loads[:first_loads]:
        copy.wait()
    loss_rows[...] = jnp.zeros_like(loss_rows)

    def chunk(step, carry):
        start = pl.multiple_of(step * CHUNK, CHUNK)
        rows = pl.ds(start, CHUNK)
        own = lax.broadcasted_iota(jnp.int32, (CHUNK, LANES), 0) + start
        hits = jnp.concatenate(
            [jnp.where(own == sampled[b : b + 1, :], 1.0, 0.0).astype(bf16) for b in range(slots)],
            axis=1,
        )
        times = jnp.dot(hits, marks[...], preferred_element_type=f32)
        pre = jnp.dot(columns[rows, :], weight_in[...], preferred_element_type=f32)
        sig = 0.5 + 0.5 * jnp.tanh(0.5 * pre)
        value = pre * sig
        hidden = value.astype(bf16)
        hiddens[rows, :] = hidden
        output = jnp.dot(hidden, weight_out[...], preferred_element_type=f32)
        predicted[rows, :] = output.astype(bf16)
        error = output - truth[rows, :].astype(f32)
        squares = jnp.sum(error * error, axis=1, keepdims=True)
        loss_rows[...] += jnp.sum((squares * times).reshape(CHUNK // 8, 8, LANES), axis=0)
        often = times[:, LANES - 1 :]
        backs[rows, :] = (often * error).astype(bf16)
        hidden_grad = lax.dot_general(
            error.astype(bf16), weight_out[...], (((1,), (1,)), ((), ())),
            preferred_element_type=f32,
        )
        pre_grads[rows, :] = (often * hidden_grad * (sig + value * (1.0 - sig))).astype(bf16)
        return carry

    lax.fori_loop(0, columns.shape[0] // CHUNK, chunk, 0)
    store(predicted, predicted_hbm)

    for tile in range(tiles):
        across = slice(tile * width, (tile + 1) * width)
        part_in = lax.dot_general(
            columns[...], pre_grads[:, across], (((0,), (0,)), ((), ())),
            preferred_element_type=f32,
        )
        part_out = lax.dot_general(
            hiddens[:, tile * height : (tile + 1) * height], backs[...], (((0,), (0,)), ((), ())),
            preferred_element_type=f32,
        )
        parts = [part_in[:, c * LANES : (c + 1) * LANES] for c in range(blocks_in)] + [part_out]
        missing = share_rows - blocks_in * feat - height
        if missing:
            parts.append(jnp.zeros((missing, LANES), f32))
        total[:, :, tile] = jnp.concatenate(parts, axis=0).reshape(
            STREAMS, trainers, piece, LANES
        )

    pl.semaphore_wait(barrier, len(friends))

    used = [0]
    pending = []

    def send(source, target, friend):
        number = used[0]
        used[0] += 1
        copy = pltpu.make_async_remote_copy(
            src_ref=source,
            dst_ref=target,
            send_sem=send_sem.at[number],
            recv_sem=recv_sem.at[number],
            device_id=friend,
            device_id_type=pl.DeviceIdType.MESH,
        )
        copy.start()
        pending.append(copy)
        return copy

    starts = [0] * STREAMS
    flying = [None] * STREAMS
    losses = loss_rows[...]
    loss_copy = None
    for step in range(train_bits):
        half = 2 ** (train_bits - 1 - step)
        if loss_copy is not None:
            loss_copy.wait_recv()
            losses = losses + loss_in[step - 1]
        loss_out[step] = losses
        loss_copy = send(loss_out.at[step], loss_in.at[step], partner(step))
        for s in range(STREAMS):
            if step:
                flying[s].wait_recv()
                total[s, pl.ds(starts[s], 2 * half)] += arrived_train[s, 2 * half : 4 * half].astype(f32)
            bit = orders[s][step]
            mine = bit_of(bit)
            away = pl.ds(starts[s] + (1 - mine) * half, half)
            outgoing[s, away] = total[s, away].astype(bf16)
            flying[s] = send(
                outgoing.at[s, away], arrived_train.at[s, pl.ds(half, half)], partner(bit)
            )
            starts[s] = starts[s] + mine * half
    tile_copies = [[] for _ in range(STREAMS)]
    for s in range(STREAMS):
        flying[s].wait_recv()
        total[s, starts[s]] += arrived_train[s, 1].astype(f32)
        for distance in range(1, tiles):
            away = (t + distance) % tiles
            outgoing[s, starts[s], away] = total[s, starts[s], away].astype(bf16)
            tile_copies[s].append(
                send(
                    outgoing.at[s, starts[s], away],
                    arrived_tile.at[s, distance],
                    other_tile(distance),
                )
            )
    loss_copy.wait_recv()
    losses = losses + loss_in[train_bits - 1]
    mine_only = lax.broadcasted_iota(jnp.int32, losses.shape, 1) == u
    trainer_loss[...] = jnp.sum(
        jnp.where(mine_only, losses, 0.0), axis=(0, 1), keepdims=True
    ) / (BLK * weight_out.shape[1])

    for copy in loads[first_loads:]:
        copy.wait()
    scale = 2.0 / BLK
    grad_copies = [None] * STREAMS
    grad_begin, begin = list(starts), list(starts)

    def pass_grads(s, step):
        size = 2 ** (train_bits - 1 - step)
        if step < train_bits - 1:
            grad_copies[s].wait_recv()
            grad_begin[s] = grad_begin[s] - bit_of(orders[s][step + 1]) * (size // 2)
        region = gathered.at[s, pl.ds(grad_begin[s], size)]
        grad_copies[s] = send(region, region, partner(orders[s][step]))

    def pass_fresh(s, step):
        size = 2 ** (train_bits - 1 - step)
        if step < train_bits - 1:
            flying[s].wait_recv()
            begin[s] = begin[s] - bit_of(orders[s][step + 1]) * (size // 2)
        region = fresh.at[s, pl.ds(begin[s], size)]
        flying[s] = send(region, region, partner(orders[s][step]))

    for s in range(STREAMS):
        done = total[s, starts[s], t]
        for distance in range(1, tiles):
            tile_copies[s][distance - 1].wait_recv()
            done = done + arrived_tile[s, distance].astype(f32)
        rounded = done.astype(bf16)
        gathered[s, starts[s]] = rounded
        rows = pl.ds(pl.multiple_of((s * trainers + starts[s]) * piece, piece), piece)
        updated, _, _ = adam_update(
            master[rows, :], moment[rows, :], second[rows, :], scale * rounded.astype(f32)
        )
        fresh[s, starts[s], t] = updated.astype(bf16)
        own = fresh.at[s, starts[s], t]
        tile_copies[s] = [send(own, own, other_tile(distance)) for distance in range(1, tiles)]
        pass_grads(s, train_bits - 1)
    for step in reversed(range(1, train_bits - 1)):
        for s in range(STREAMS):
            pass_grads(s, step)
    for s in range(STREAMS):
        for copy in tile_copies[s]:
            copy.wait_recv()
        pass_fresh(s, train_bits - 1)
    for s in range(STREAMS):
        pass_grads(s, 0)
    for s in range(STREAMS):
        grad_copies[s].wait_recv()
    for s in range(STREAMS):
        for q in range(trainers):
            first = (s * trainers + q) * piece
            rows = slice(first, first + piece)
            changed = adam_update(
                master[rows, :], moment[rows, :], second[rows, :],
                scale * gathered[s, q].astype(f32),
            )
            master[rows, :], moment[rows, :], second[rows, :] = changed
    for inner, outer, flat in (
        (new_master_in, new_master_out, master),
        (new_moment_in, new_moment_out, moment),
        (new_second_in, new_second_out, second),
    ):
        for c in range(blocks_in):
            store(flat.at[pl.ds(c * feat, feat)], inner.at[:, pl.ds(c * LANES, LANES)])
        store(flat.at[pl.ds(end_in, height)], outer)
    for step in reversed(range(train_bits - 1)):
        for s in range(STREAMS):
            pass_fresh(s, step)
    for s in range(STREAMS):
        flying[s].wait_recv()
    for tile in range(tiles):
        flat = fresh[:, :, tile].reshape(share_rows, LANES)
        for c in range(blocks_in):
            left = tile * width + c * LANES
            fresh_in[:, left : left + LANES] = flat[c * feat : (c + 1) * feat]
        fresh_out[tile * height : (tile + 1) * height, :] = flat[end_in : end_in + height]
    store(fresh_in, fresh_in_hbm)
    store(fresh_out, fresh_out_hbm)
    for copy in pending:
        copy.wait_send()
    for copy in stores:
        copy.wait()


def store_kernel(*refs):
    count = (len(refs) - 1) // 2
    sources, targets, sem = refs[:count], refs[count:-1], refs[-1]
    copies = []
    for number in range(count):
        if number != 1:
            copy = pltpu.make_async_copy(sources[number], targets[number], sem.at[number])
            copy.start()
            copies.append(copy)
    targets[1][...] = sources[1][...]
    for copy in copies:
        copy.wait()


def local(
    columns, truth, weight_in, weight_out,
    master_in, master_out, moment_in, moment_out, second_in, second_out,
    counts, sampled, routes,
):
    tiles, trainers = lax.axis_size("tile"), lax.axis_size("train")
    train_bits = bits_of(trainers)
    rows, feat = columns.shape
    hidden, outs = weight_out.shape
    slots = sampled.shape[0]
    needed = (feat * master_in.shape[1] + master_out.shape[0] * outs) // LANES
    piece = -(-needed // (STREAMS * trainers * 16)) * 16
    copies = STREAMS * (3 * train_bits + 2 * (tiles - 1)) + train_bits
    blocks_in = master_in.shape[1] // LANES
    flat = (STREAMS * trainers * piece, LANES)
    vmem, hbm = pl.BlockSpec(memory_space=pltpu.VMEM), pl.BlockSpec(memory_space=pltpu.HBM)
    smem = pl.BlockSpec(memory_space=pltpu.SMEM)
    like = lambda a: jax.ShapeDtypeStruct(a.shape, a.dtype)
    results = pl.pallas_call(
        functools.partial(kernel, tiles, trainers),
        out_shape=(
            like(truth),
            jax.ShapeDtypeStruct((1, 1), f32),
            like(weight_in),
            like(weight_out),
            like(master_in), like(master_out),
            like(moment_in), like(moment_out),
            like(second_in), like(second_out),
        ),
        in_specs=[hbm] * 11 + [smem] * 2,
        out_specs=(hbm, vmem) + (hbm,) * 8,
        scratch_shapes=[
            pltpu.VMEM(columns.shape, bf16),
            pltpu.VMEM(truth.shape, bf16),
            pltpu.VMEM(weight_in.shape, bf16),
            pltpu.VMEM(weight_out.shape, bf16),
            pltpu.VMEM(sampled.shape, jnp.int32),
            pltpu.VMEM(flat, f32),
            pltpu.VMEM(flat, f32),
            pltpu.VMEM(flat, f32),
            pltpu.VMEM(truth.shape, bf16),
            pltpu.VMEM(weight_in.shape, bf16),
            pltpu.VMEM(weight_out.shape, bf16),
            pltpu.VMEM((slots * BLK, LANES), bf16),
            pltpu.VMEM((rows, hidden), bf16),
            pltpu.VMEM((rows, hidden), bf16),
            pltpu.VMEM((rows, outs), bf16),
            pltpu.VMEM((8, LANES), f32),
            pltpu.VMEM((STREAMS, trainers, tiles, piece, LANES), f32),
            pltpu.VMEM((STREAMS, trainers, tiles, piece, LANES), bf16),
            pltpu.VMEM((STREAMS, trainers, tiles, piece, LANES), bf16),
            pltpu.VMEM((STREAMS, tiles, piece, LANES), bf16),
            pltpu.VMEM((STREAMS, trainers, piece, LANES), bf16),
            pltpu.VMEM((STREAMS, trainers, tiles, piece, LANES), bf16),
            pltpu.VMEM((train_bits, 8, LANES), f32),
            pltpu.VMEM((train_bits, 8, LANES), f32),
            pltpu.SemaphoreType.DMA((copies,)),
            pltpu.SemaphoreType.DMA((copies,)),
            pltpu.SemaphoreType.DMA((5 + 3 * (blocks_in + 1),)),
            pltpu.SemaphoreType.DMA((3 + 3 * (blocks_in + 1),)),
        ],
        compiler_params=pltpu.CompilerParams(
            collective_id=0, has_side_effects=True, vmem_limit_bytes=59 * 2**20
        ),
    )(
        columns, truth, weight_in, weight_out,
        master_in, master_out, moment_in, moment_out, second_in, second_out,
        sampled, counts, routes.reshape(1, slots),
    )
    stored = pl.pallas_call(
        store_kernel,
        out_shape=(
            like(truth),
            jax.ShapeDtypeStruct((1, 1), f32),
            like(weight_in), like(weight_out),
            like(master_in), like(master_out),
            like(moment_in), like(moment_out),
            like(second_in), like(second_out),
        ),
        in_specs=[hbm, vmem] + [hbm] * 8,
        out_specs=(hbm, vmem) + (hbm,) * 8,
        scratch_shapes=[pltpu.SemaphoreType.DMA((10,))],
        compiler_params=pltpu.CompilerParams(vmem_limit_bytes=59 * 2**20),
    )(*results)
    return (stored[0], stored[1].reshape(1)) + tuple(stored[2:])


def solution(mesh):
    return jax.shard_map(
        local,
        mesh=mesh,
        in_specs=(
            P(("tile", "train"), None),
            P(("tile", "train"), None),
            P(),
            P(),
            P(None, "tile"),
            P("tile", None),
            P(None, "tile"),
            P("tile", None),
            P(None, "tile"),
            P("tile", None),
            P(("tile", "train")),
            P(("tile", "train"), None),
            P(("tile", "train"), None),
        ),
        out_specs=(
            P(("tile", "train"), None),
            P(("tile", "train")),
            P(),
            P(),
            P(None, "tile"),
            P("tile", None),
            P(None, "tile"),
            P("tile", None),
            P(None, "tile"),
            P("tile", None),
        ),
        check_vma=False,
    )
```

```python
import functools
import jax
import jax.numpy as jnp
from jax import lax
from jax.experimental import pallas as pl
from jax.experimental.pallas import tpu as pltpu
from jax.sharding import PartitionSpec as P

BLK = 128
LANES = 128
STREAMS = 2
CHUNK = 256

rate = 0.001
first_fix = 1.0 - 0.9**8
second_fix = 1.0 - 0.999**8
f32, bf16 = jnp.float32, jnp.bfloat16


def adam_update(master, moment, second, grad):
    moment = 0.9 * moment + 0.1 * grad
    second = 0.999 * second + 0.001 * grad * grad
    master = master - rate * (moment / first_fix) / (jnp.sqrt(second / second_fix) + 1e-08)
    return (master, moment, second)


def bits_of(size):
    return size.bit_length() - 1


def stream_orders(trainers):
    ascending = list(range(bits_of(trainers)))
    return [ascending, ascending[:1] + ascending[:0:-1]]


def kernel(
    tiles, trainers,
    columns_hbm, truth_hbm, weight_in_hbm, weight_out_hbm,
    master_in, master_out, moment_in, moment_out, second_in, second_out,
    sampled_hbm, counts, routes,
    predicted_hbm, trainer_loss, fresh_in_hbm, fresh_out_hbm,
    new_master_in, new_master_out, new_moment_in, new_moment_out, new_second_in, new_second_out,
    columns, truth, weight_in, weight_out, sampled, master, moment, second,
    predicted, fresh_in, fresh_out,
    marks, pre_grads, hiddens, backs, loss_rows,
    total, outgoing, arrived_train, arrived_tile, gathered, fresh, loss_out, loss_in,
    send_sem, recv_sem, load_sem, store_sem,
):
    t, u = lax.axis_index("tile"), lax.axis_index("train")
    train_bits = bits_of(trainers)
    orders = stream_orders(trainers)
    piece = total.shape[3]
    share_rows = STREAMS * trainers * piece
    feat, width = master_in.shape
    height = master_out.shape[0]
    blocks_in = width // LANES

    def load(source, target):
        copy = pltpu.make_async_copy(source, target, load_sem.at[len(loads)])
        copy.start()
        loads.append(copy)

    def store(source, target):
        copy = pltpu.make_async_copy(source, target, store_sem.at[len(stores)])
        copy.start()
        stores.append(copy)

    loads, stores = [], []
    load(sampled_hbm, sampled)
    load(columns_hbm, columns)
    load(weight_in_hbm, weight_in)
    load(weight_out_hbm, weight_out)
    load(truth_hbm, truth)
    first_loads = len(loads)
    end_in = blocks_in * feat
    for inner, outer, flat in (
        (master_in, master_out, master), (moment_in, moment_out, moment), (second_in, second_out, second)
    ):
        for c in range(blocks_in):
            load(inner.at[:, pl.ds(c * LANES, LANES)], flat.at[pl.ds(c * feat, feat)])
        load(outer, flat.at[pl.ds(end_in, height)])
        if end_in + height < share_rows:
            missing = share_rows - end_in - height
            flat[end_in + height :, :] = jnp.zeros((missing, LANES), f32)

    def bit_of(bit):
        return (u // 2**bit) % 2

    def partner(bit):
        return {"train": u + 2**bit * (1 - 2 * bit_of(bit))}

    def other_tile(distance):
        return {"tile": (t + distance) % tiles}

    friends = [partner(bit) for bit in range(train_bits)]
    friends += [other_tile(distance) for distance in range(1, tiles)]
    barrier = pltpu.get_barrier_semaphore()
    for friend in friends:
        pl.semaphore_signal(
            barrier, inc=1, device_id=friend, device_id_type=pl.DeviceIdType.MESH
        )

    slots = sampled.shape[0]
    lane = lax.broadcasted_iota(jnp.int32, (BLK, LANES), 1)
    for b in range(slots):
        named = (lane >= trainers) | (lane == routes[0, b])
        named = named & (counts[0] > b)
        marks[b * BLK : (b + 1) * BLK, :] = jnp.where(named, 1.0, 0.0).astype(bf16)
    for copy in loads[:first_loads]:
        copy.wait()
    loss_rows[...] = jnp.zeros_like(loss_rows)

    def chunk(step, carry):
        start = pl.multiple_of(step * CHUNK, CHUNK)
        rows = pl.ds(start, CHUNK)
        own = lax.broadcasted_iota(jnp.int32, (CHUNK, LANES), 0) + start
        hits = jnp.concatenate(
            [jnp.where(own == sampled[b : b + 1, :], 1.0, 0.0).astype(bf16) for b in range(slots)],
            axis=1,
        )
        times = jnp.dot(hits, marks[...], preferred_element_type=f32)
        pre = jnp.dot(columns[rows, :], weight_in[...], preferred_element_type=f32)
        sig = 0.5 + 0.5 * jnp.tanh(0.5 * pre)
        value = pre * sig
        hidden = value.astype(bf16)
        hiddens[rows, :] = hidden
        output = jnp.dot(hidden, weight_out[...], preferred_element_type=f32)
        predicted[rows, :] = output.astype(bf16)
        error = output - truth[rows, :].astype(f32)
        squares = jnp.sum(error * error, axis=1, keepdims=True)
        loss_rows[...] += jnp.sum((squares * times).reshape(CHUNK // 8, 8, LANES), axis=0)
        often = times[:, LANES - 1 :]
        backs[rows, :] = (often * error).astype(bf16)
        hidden_grad = lax.dot_general(
            error.astype(bf16), weight_out[...], (((1,), (1,)), ((), ())),
            preferred_element_type=f32,
        )
        pre_grads[rows, :] = (often * hidden_grad * (sig + value * (1.0 - sig))).astype(bf16)
        return carry

    lax.fori_loop(0, columns.shape[0] // CHUNK, chunk, 0)
    store(predicted, predicted_hbm)

    for tile in range(tiles):
        across = slice(tile * width, (tile + 1) * width)
        part_in = lax.dot_general(
            columns[...], pre_grads[:, across], (((0,), (0,)), ((), ())),
            preferred_element_type=f32,
        )
        part_out = lax.dot_general(
            hiddens[:, tile * height : (tile + 1) * height], backs[...], (((0,), (0,)), ((), ())),
            preferred_element_type=f32,
        )
        parts = [part_in[:, c * LANES : (c + 1) * LANES] for c in range(blocks_in)] + [part_out]
        missing = share_rows - blocks_in * feat - height
        if missing:
            parts.append(jnp.zeros((missing, LANES), f32))
        total[:, :, tile] = jnp.concatenate(parts, axis=0).reshape(
            STREAMS, trainers, piece, LANES
        )

    pl.semaphore_wait(barrier, len(friends))

    used = [0]
    pending = []

    def send(source, target, friend):
        number = used[0]
        used[0] += 1
        copy = pltpu.make_async_remote_copy(
            src_ref=source,
            dst_ref=target,
            send_sem=send_sem.at[number],
            recv_sem=recv_sem.at[number],
            device_id=friend,
            device_id_type=pl.DeviceIdType.MESH,
        )
        copy.start()
        pending.append(copy)
        return copy

    starts = [0] * STREAMS
    flying = [None] * STREAMS
    losses = loss_rows[...]
    loss_copy = None
    for step in range(train_bits):
        half = 2 ** (train_bits - 1 - step)
        if loss_copy is not None:
            loss_copy.wait_recv()
            losses = losses + loss_in[step - 1]
        loss_out[step] = losses
        loss_copy = send(loss_out.at[step], loss_in.at[step], partner(step))
        for s in range(STREAMS):
            if step:
                flying[s].wait_recv()
                total[s, pl.ds(starts[s], 2 * half)] += arrived_train[s, 2 * half : 4 * half].astype(f32)
            bit = orders[s][step]
            mine = bit_of(bit)
            away = pl.ds(starts[s] + (1 - mine) * half, half)
            outgoing[s, away] = total[s, away].astype(bf16)
            flying[s] = send(
                outgoing.at[s, away], arrived_train.at[s, pl.ds(half, half)], partner(bit)
            )
            starts[s] = starts[s] + mine * half
    tile_copies = [[] for _ in range(STREAMS)]
    for s in range(STREAMS):
        flying[s].wait_recv()
        total[s, starts[s]] += arrived_train[s, 1].astype(f32)
        for distance in range(1, tiles):
            away = (t + distance) % tiles
            outgoing[s, starts[s], away] = total[s, starts[s], away].astype(bf16)
            tile_copies[s].append(
                send(
                    outgoing.at[s, starts[s], away],
                    arrived_tile.at[s, distance],
                    other_tile(distance),
                )
            )
    loss_copy.wait_recv()
    losses = losses + loss_in[train_bits - 1]
    mine_only = lax.broadcasted_iota(jnp.int32, losses.shape, 1) == u
    trainer_loss[...] = jnp.sum(
        jnp.where(mine_only, losses, 0.0), axis=(0, 1), keepdims=True
    ) / (BLK * weight_out.shape[1])

    for copy in loads[first_loads:]:
        copy.wait()
    scale = 2.0 / BLK
    grad_copies = [None] * STREAMS
    grad_begin, begin = list(starts), list(starts)

    def pass_grads(s, step):
        size = 2 ** (train_bits - 1 - step)
        if step < train_bits - 1:
            grad_copies[s].wait_recv()
            grad_begin[s] = grad_begin[s] - bit_of(orders[s][step + 1]) * (size // 2)
        region = gathered.at[s, pl.ds(grad_begin[s], size)]
        grad_copies[s] = send(region, region, partner(orders[s][step]))

    def pass_fresh(s, step):
        size = 2 ** (train_bits - 1 - step)
        if step < train_bits - 1:
            flying[s].wait_recv()
            begin[s] = begin[s] - bit_of(orders[s][step + 1]) * (size // 2)
        region = fresh.at[s, pl.ds(begin[s], size)]
        flying[s] = send(region, region, partner(orders[s][step]))

    for s in range(STREAMS):
        done = total[s, starts[s], t]
        for distance in range(1, tiles):
            tile_copies[s][distance - 1].wait_recv()
            done = done + arrived_tile[s, distance].astype(f32)
        rounded = done.astype(bf16)
        gathered[s, starts[s]] = rounded
        rows = pl.ds(pl.multiple_of((s * trainers + starts[s]) * piece, piece), piece)
        updated, _, _ = adam_update(
            master[rows, :], moment[rows, :], second[rows, :], scale * rounded.astype(f32)
        )
        fresh[s, starts[s], t] = updated.astype(bf16)
        own = fresh.at[s, starts[s], t]
        tile_copies[s] = [send(own, own, other_tile(distance)) for distance in range(1, tiles)]
        pass_grads(s, train_bits - 1)
    for step in reversed(range(1, train_bits - 1)):
        for s in range(STREAMS):
            pass_grads(s, step)
    for s in range(STREAMS):
        for copy in tile_copies[s]:
            copy.wait_recv()
        pass_fresh(s, train_bits - 1)
    for s in range(STREAMS):
        pass_grads(s, 0)
    for s in range(STREAMS):
        grad_copies[s].wait_recv()
    for s in range(STREAMS):
        for q in range(trainers):
            first = (s * trainers + q) * piece
            rows = slice(first, first + piece)
            changed = adam_update(
                master[rows, :], moment[rows, :], second[rows, :],
                scale * gathered[s, q].astype(f32),
            )
            master[rows, :], moment[rows, :], second[rows, :] = changed
    for inner, outer, flat in (
        (new_master_in, new_master_out, master),
        (new_moment_in, new_moment_out, moment),
        (new_second_in, new_second_out, second),
    ):
        for c in range(blocks_in):
            store(flat.at[pl.ds(c * feat, feat)], inner.at[:, pl.ds(c * LANES, LANES)])
        store(flat.at[pl.ds(end_in, height)], outer)
    for step in reversed(range(train_bits - 1)):
        for s in range(STREAMS):
            pass_fresh(s, step)
    for s in range(STREAMS):
        flying[s].wait_recv()
    for tile in range(tiles):
        flat = fresh[:, :, tile].reshape(share_rows, LANES)
        for c in range(blocks_in):
            left = tile * width + c * LANES
            fresh_in[:, left : left + LANES] = flat[c * feat : (c + 1) * feat]
        fresh_out[tile * height : (tile + 1) * height, :] = flat[end_in : end_in + height]
    store(fresh_in, fresh_in_hbm)
    store(fresh_out, fresh_out_hbm)
    for copy in pending:
        copy.wait_send()
    for copy in stores:
        copy.wait()


def store_kernel(*refs):
    count = (len(refs) - 2) // 3
    sources, targets, held = refs[:count], refs[count : 2 * count], refs[2 * count : 3 * count]
    load_sem, store_sem = refs[-2:]
    moved = [number for number in range(count) if number != 1]
    loads = [
        pltpu.make_async_copy(sources[number], held[number], load_sem.at[number]) for number in moved
    ]
    stores = [
        pltpu.make_async_copy(held[number], targets[number], store_sem.at[number]) for number in moved
    ]
    for copy in loads:
        copy.start()
    targets[1][...] = sources[1][...]
    for first, second in zip(loads, stores):
        first.wait()
        second.start()
    for copy in stores:
        copy.wait()


def local(
    columns, truth, weight_in, weight_out,
    master_in, master_out, moment_in, moment_out, second_in, second_out,
    counts, sampled, routes,
):
    tiles, trainers = lax.axis_size("tile"), lax.axis_size("train")
    train_bits = bits_of(trainers)
    rows, feat = columns.shape
    hidden, outs = weight_out.shape
    slots = sampled.shape[0]
    needed = (feat * master_in.shape[1] + master_out.shape[0] * outs) // LANES
    piece = -(-needed // (STREAMS * trainers * 16)) * 16
    copies = STREAMS * (3 * train_bits + 2 * (tiles - 1)) + train_bits
    blocks_in = master_in.shape[1] // LANES
    flat = (STREAMS * trainers * piece, LANES)
    vmem, hbm = pl.BlockSpec(memory_space=pltpu.VMEM), pl.BlockSpec(memory_space=pltpu.HBM)
    smem = pl.BlockSpec(memory_space=pltpu.SMEM)
    like = lambda a: jax.ShapeDtypeStruct(a.shape, a.dtype)
    results = pl.pallas_call(
        functools.partial(kernel, tiles, trainers),
        out_shape=(
            like(truth),
            jax.ShapeDtypeStruct((1, 1), f32),
            like(weight_in),
            like(weight_out),
            like(master_in), like(master_out),
            like(moment_in), like(moment_out),
            like(second_in), like(second_out),
        ),
        in_specs=[hbm] * 11 + [smem] * 2,
        out_specs=(hbm, vmem) + (hbm,) * 8,
        scratch_shapes=[
            pltpu.VMEM(columns.shape, bf16),
            pltpu.VMEM(truth.shape, bf16),
            pltpu.VMEM(weight_in.shape, bf16),
            pltpu.VMEM(weight_out.shape, bf16),
            pltpu.VMEM(sampled.shape, jnp.int32),
            pltpu.VMEM(flat, f32),
            pltpu.VMEM(flat, f32),
            pltpu.VMEM(flat, f32),
            pltpu.VMEM(truth.shape, bf16),
            pltpu.VMEM(weight_in.shape, bf16),
            pltpu.VMEM(weight_out.shape, bf16),
            pltpu.VMEM((slots * BLK, LANES), bf16),
            pltpu.VMEM((rows, hidden), bf16),
            pltpu.VMEM((rows, hidden), bf16),
            pltpu.VMEM((rows, outs), bf16),
            pltpu.VMEM((8, LANES), f32),
            pltpu.VMEM((STREAMS, trainers, tiles, piece, LANES), f32),
            pltpu.VMEM((STREAMS, trainers, tiles, piece, LANES), bf16),
            pltpu.VMEM((STREAMS, trainers, tiles, piece, LANES), bf16),
            pltpu.VMEM((STREAMS, tiles, piece, LANES), bf16),
            pltpu.VMEM((STREAMS, trainers, piece, LANES), bf16),
            pltpu.VMEM((STREAMS, trainers, tiles, piece, LANES), bf16),
            pltpu.VMEM((train_bits, 8, LANES), f32),
            pltpu.VMEM((train_bits, 8, LANES), f32),
            pltpu.SemaphoreType.DMA((copies,)),
            pltpu.SemaphoreType.DMA((copies,)),
            pltpu.SemaphoreType.DMA((5 + 3 * (blocks_in + 1),)),
            pltpu.SemaphoreType.DMA((3 + 3 * (blocks_in + 1),)),
        ],
        compiler_params=pltpu.CompilerParams(
            collective_id=0, has_side_effects=True, vmem_limit_bytes=59 * 2**20
        ),
    )(
        columns, truth, weight_in, weight_out,
        master_in, master_out, moment_in, moment_out, second_in, second_out,
        sampled, counts, routes.reshape(1, slots),
    )
    stored = pl.pallas_call(
        store_kernel,
        out_shape=(
            like(truth),
            jax.ShapeDtypeStruct((1, 1), f32),
            like(weight_in), like(weight_out),
            like(master_in), like(master_out),
            like(moment_in), like(moment_out),
            like(second_in), like(second_out),
        ),
        in_specs=[hbm, vmem] + [hbm] * 8,
        out_specs=(hbm, vmem) + (hbm,) * 8,
        scratch_shapes=[pltpu.VMEM(a.shape, a.dtype) for a in results]
        + [pltpu.SemaphoreType.DMA((len(results),))] * 2,
        compiler_params=pltpu.CompilerParams(vmem_limit_bytes=59 * 2**20),
    )(*results)
    return (stored[0], stored[1].reshape(1)) + tuple(stored[2:])


def solution(mesh):
    return jax.shard_map(
        local,
        mesh=mesh,
        in_specs=(
            P(("tile", "train"), None),
            P(("tile", "train"), None),
            P(),
            P(),
            P(None, "tile"),
            P("tile", None),
            P(None, "tile"),
            P("tile", None),
            P(None, "tile"),
            P("tile", None),
            P(("tile", "train")),
            P(("tile", "train"), None),
            P(("tile", "train"), None),
        ),
        out_specs=(
            P(("tile", "train"), None),
            P(("tile", "train")),
            P(),
            P(),
            P(None, "tile"),
            P("tile", None),
            P(None, "tile"),
            P("tile", None),
            P(None, "tile"),
            P("tile", None),
        ),
        check_vma=False,
    )
```
